256 devices in a mesh: cols: 64 (over x, z, y_hi), sec: 4 (over y_lo, core).
Axes of the slice: x: 4, y: 4 (y_hi: 2, y_lo: 2; y = y_hi * 2 + y_lo), z: 8, core: 2. Of those that a mesh axis runs over, the one named last changes fastest.
Arguments:
- trial: float32 [128, 16, 96, 512], P('cols', None, None, 'sec'), may hold values from -6 to 6
- orbitals: float32 [64, 16, 96, 512], P('cols', None, None, 'sec'), may hold values from -6 to 6
- potential: float32 [16, 96, 512], P(None, None, 'sec'), may hold values from -4 to 4
- owner: int32 [2], replicated, may hold values from 0 to 63
Outputs:
- response: float32 [128, 16, 96, 512], P('cols', None, None, 'sec')
The draws below stay inside these ranges and needn't reach their ends.
All inputs are finite; a program needn't handle non-finite values.
Results may differ from the reference program's by a relative error of at most 0.00002.
Values sent between devices are 32-bit elements; how exact they have to be, the bound alone decides.
A program may use at most 64 MiB of HBM per device.

```python
import jax
import jax.numpy as jnp
from jax import lax

NY = 16
NZ = 96
ROUNDS = 2
COLUMNS = 128
SLOTS = 64
NX = 512
N_COLS = 64


def levels(own_key, extent, shards, low, largest):
    loudness = 1.0
    for position, shards_of in shards:
        heights = jax.random.uniform(jax.random.fold_in(jax.random.fold_in(own_key, 6), position), (shards_of,), jnp.float32, low / len(shards), largest / len(shards))
        loudness = loudness * jnp.repeat(jnp.exp(heights), extent[position] // shards_of).reshape((-1,) + (1,) * (len(extent) - 1 - position))
    return loudness


def centred(stream_key, shape, width, bound, split=(), kind=jnp.bfloat16):
    factor_of = levels(stream_key, shape, split, -0.22, 0.18) if split else 1.0
    array = jax.random.normal(stream_key, shape, jnp.float32) * width * factor_of
    return jnp.minimum(jnp.maximum(array, -bound), bound).astype(kind)


def setup_inputs(seed: int = 0) -> dict:
    keys = jax.random.split(jax.random.key(seed), 5)
    return {
        "trial": centred(keys[0], (COLUMNS, NY, NZ, NX), 1.0, 6.0, ((0, 64), (3, 4)), jnp.float32),
        "orbitals": centred(keys[1], (SLOTS, NY, NZ, NX), 1.0, 6.0, ((0, 64), (3, 4)), jnp.float32),
        "potential": jnp.clip(jax.random.uniform(keys[2], (NY, NZ, NX), jnp.float32, -4.0, 4.0) * levels(keys[2], (NY, NZ, NX), ((2, 4),), -0.4, 0.0), -4.0, 4.0),
        "owner": jax.random.randint(keys[3], (ROUNDS,), 0, N_COLS).astype(jnp.int32),
    }


grid_step = 0.5
spectrum_mid = 16.0
spectrum_half = 20.0
occupation = 2.0
weight_zero = 0.4
weight_one = -0.5
weight_two = 0.3
weight_three = -0.25


def apply_scaled(extended, potential):
    center = extended[..., 2:-2]
    diag_coef = -30.0 / 12.0
    near_coef = 16.0 / 12.0
    far_coef = -1.0 / 12.0
    along_x = diag_coef * center + near_coef * (extended[..., 3:-1] + extended[..., 1:-3]) + far_coef * (extended[..., 4:] + extended[..., :-4])
    leading = center.ndim - 3
    padded = jnp.pad(center, [(0, 0)] * leading + [(2, 2), (2, 2), (0, 0)])
    along_y = diag_coef * center + near_coef * (padded[..., 3:-1, 2:-2, :] + padded[..., 1:-3, 2:-2, :]) + far_coef * (padded[..., 4:, 2:-2, :] + padded[..., :-4, 2:-2, :])
    along_z = diag_coef * center + near_coef * (padded[..., 2:-2, 3:-1, :] + padded[..., 2:-2, 1:-3, :]) + far_coef * (padded[..., 2:-2, 4:, :] + padded[..., 2:-2, :-4, :])
    kinetic = -0.5 * (along_x + along_y + along_z) / (grid_step * grid_step)
    return (kinetic + potential * center - spectrum_mid * center) / spectrum_half


def wrapped(field):
    return jnp.concatenate([field[..., -2:], field, field[..., :2]], axis=-1)


def reference(trial, orbitals, potential, owner):
    def one_column(column):
        total = jnp.zeros_like(column)
        for turn in range(ROUNDS):
            orbital = orbitals[owner[turn]]
            first = orbital * column
            second = apply_scaled(wrapped(first), potential)
            third = 2.0 * apply_scaled(wrapped(second), potential) - first
            fourth = 2.0 * apply_scaled(wrapped(third), potential) - second
            filtered = weight_zero * first + weight_one * second + weight_two * third + weight_three * fourth
            total = total + occupation * orbital * filtered
        return total

    return lax.map(one_column, trial)
```

```python
import functools

import jax
import jax.numpy as jnp
from jax import lax
from jax.experimental import pallas as pl
from jax.experimental.pallas import tpu as pltpu
from jax.sharding import PartitionSpec as P

MESH = pl.DeviceIdType.MESH
F32 = jnp.float32

ROUNDS = 2
X, Z, H = 4, 8, 2
PAD = 16
HALO = 8


def coords(index):
    return index // (Z * H), (index // H) % Z, index % H


def at(x, z, h):
    return (x * Z + z) * H + h


def pick(select, yes, no):
    return jnp.where(jnp.full(yes.shape, select, jnp.int32) != 0, yes, no)


class Ring:
    def __init__(self, name, me):
        x, z, h = me
        self.name = name
        self.size = {"x": X, "z": Z}[name]
        self.me = {"x": x, "z": z}[name]

        def move(step):
            if name == "x":
                return at((x + step + X) % X, z, h)
            return at(x, (z + step + Z) % Z, h)

        self.right, self.left = move(1), move(-1)


class Sems:
    def __init__(self, send, recv):
        self.send, self.recv, self.count = send, recv, 0

    def take(self):
        self.count += 1
        return self.send.at[self.count - 1], self.recv.at[self.count - 1]


def remote(src, dst, sems, cols, sec):
    send, recv = sems.take()
    return pltpu.make_async_remote_copy(
        src_ref=src, dst_ref=dst, send_sem=send, recv_sem=recv, device_id=(cols, sec), device_id_type=MESH
    )


def rows(ref, start, size):
    return ref.at[pl.ds(pl.multiple_of(start, 8), size), :]


def spread(own, base, size, out, slots, first, second, me, root, flip, sems, sent):
    sec = lax.axis_index("sec")
    x, z, h = me
    taken = [0]

    def slot(n):
        taken[0] += n
        return slots.at[pl.ds(taken[0] - n, n), :]

    def go(src, dst, cols):
        copy = remote(src, dst, sems, cols, sec)
        copy.start()
        sent.append(copy)
        return copy

    def counts(ring):
        more, fewer = ring.size // 2, (ring.size - 1) // 2
        return (fewer, more) if flip else (more, fewer)

    def scatter(src, offset, piece, ring, root_at):
        n, i = ring.size, ring.me
        n_right, n_left = counts(ring)
        mine = jnp.where(root_at == i, 1, 0)
        right = left = None
        for step in range(1, max(n_right, n_left) + 1):
            for way, last, target in ((1, n_right, ring.right), (-1, n_left, ring.left)):
                if step > last:
                    continue
                held = right if way == 1 else left
                which = (i + way * (last + 1 - step) + n) % n
                source = rows(src, offset + which * piece, piece)
                if step > 1:
                    held[1].wait_recv()
                    merged = slot(piece)
                    merged[...] = pick(mine, source[...], held[0][...])
                    source = merged
                landing = slot(piece)
                copy = go(source, landing, target)
                if way == 1:
                    right = (landing, copy)
                else:
                    left = (landing, copy)
            yield None
        value = rows(src, offset + i * piece, piece)[...]
        behind = (i - root_at + n) % n
        if right is not None:
            right[1].wait_recv()
            value = pick(jnp.where((behind >= 1) & (behind <= n_right), 1, 0), right[0][...], value)
        if left is not None:
            left[1].wait_recv()
            value = pick(jnp.where(behind > n_right, 1, 0), left[0][...], value)
        yield value

    def gather(offset, piece, ring):
        n, i = ring.size, ring.me
        n_right, n_left = counts(ring)
        copies = {}
        for step in range(1, max(n_right, n_left) + 1):
            for way, last, target in ((1, n_right, ring.right), (-1, n_left, ring.left)):
                if step > last:
                    continue
                if step > 1:
                    copies[way].wait_recv()
                which = (i - way * (step - 1) + n) % n
                place = rows(out, offset + which * piece, piece)
                copies[way] = go(place, place, target)
            yield
        for copy in copies.values():
            copy.wait_recv()

    piece1 = size // first.size
    piece2 = piece1 // second.size
    root_x, root_z, root_h = root
    root1, root2 = (root_z, root_x) if first.name == "z" else (root_x, root_z)

    value = None
    for value in scatter(own, base, piece1, first, root1):
        if value is None:
            yield
    held = slot(piece1)
    held[...] = value
    for value in scatter(held, 0, piece2, second, root2):
        if value is None:
            yield
    place = base + first.me * piece1 + second.me * piece2
    final = rows(out, place, piece2)
    if H > 1:
        mid, landing = slot(piece2), slot(piece2)
        mid[...] = value
        copy = go(mid, landing, at(x, z, (h + 1) % H))
        yield
        copy.wait_recv()
        value = pick(jnp.where(root_h == h, 1, 0), value, landing[...])
    final[...] = value
    yield from gather(base + first.me * piece1, piece2, second)
    yield from gather(base, piece1, first)


def slot_rows(size):
    def one(n, piece):
        return (2 * (n - 1)) * piece

    a = one(Z, size // Z) + size // Z + one(X, size // (Z * X)) + 2 * size // (Z * X)
    b = one(X, size // X) + size // X + one(Z, size // (Z * X)) + 2 * size // (Z * X)
    return max(a, b)


def turned(plane, nz):
    return jnp.concatenate([plane, jnp.zeros((128 - nz, 128), F32)], axis=0).T


def stencil(src, d_ref, y, ny, row):
    def read(plane, shift):
        return src[plane, pl.ds(row + shift, 8), :]

    u = read(y, 0)
    near = read(y, 1) + read(y, -1)
    far = read(y, 2) + read(y, -2)
    near = near + (pltpu.roll(u, 1, 1) + pltpu.roll(u, 127, 1))
    far = far + (pltpu.roll(u, 2, 1) + pltpu.roll(u, 126, 1))
    for shift in (-1, 1):
        if 0 <= y + shift < ny:
            near = near + read(y + shift, 0)
    for shift in (-2, 2):
        if 0 <= y + shift < ny:
            far = far + read(y + shift, 0)
    return (far - 16.0 * near) + d_ref[y, pl.ds(row, 8), :] * u


def kernel(
    owner_ref, trial_ref, orbital_ref, potential_ref, out_ref,
    trial_v, orbital_v, potential_v, psi, slots, psi_t, trial_t, d_t, w, u1, u2, total, out_v,
    load_sem, store_sem, send_sem, recv_sem,
):
    ny, nz, nx = potential_v.shape
    n_rows = ny * nz
    sec = lax.axis_index("sec")
    n_sec = lax.axis_size("sec")
    cols = lax.axis_index("cols")
    me = coords(cols)
    x, z, h = me
    ring_x, ring_z = Ring("x", me), Ring("z", me)
    sec_right, sec_left = (sec + 1) % n_sec, (sec + n_sec - 1) % n_sec

    loads = [
        pltpu.make_async_copy(orbital_ref.at[0], orbital_v, load_sem.at[0]),
        pltpu.make_async_copy(trial_ref, trial_v, load_sem.at[1]),
        pltpu.make_async_copy(potential_ref, potential_v, load_sem.at[2]),
    ]
    for load in loads:
        load.start()

    barrier = pltpu.get_barrier_semaphore()
    partners = [(ring_x.right, sec), (ring_x.left, sec), (ring_z.right, sec), (ring_z.left, sec)]
    if H > 1:
        partners.append((at(x, z, (h + 1) % H), sec))
    partners += [(cols, sec_right), (cols, sec_left)]
    for partner in partners:
        pl.semaphore_signal(barrier, inc=1, device_id=partner, device_id_type=MESH)
    pl.semaphore_wait(barrier, len(partners))

    sems = Sems(send_sem, recv_sem)
    sent = []
    loads[0].wait()

    half = n_rows // 2
    parts = []
    for turn in range(ROUNDS):
        root = coords(owner_ref[turn])
        for part, (first, second) in enumerate(((ring_z, ring_x), (ring_x, ring_z))):
            parts.append(
                spread(
                    orbital_v, part * half, half, psi.at[turn], slots.at[2 * turn + part],
                    first, second, me, root, turn == 1, sems, sent,
                )
            )

    def advance(which):
        for part in which:
            next(part, None)

    def swap_edges(ref, lead):
        every = (slice(None),) * lead
        first = ref.at[every + (pl.ds(PAD, HALO),)]
        last = ref.at[every + (pl.ds(PAD + nx - HALO, HALO),)]
        before = ref.at[every + (pl.ds(PAD - HALO, HALO),)]
        after = ref.at[every + (pl.ds(PAD + nx, HALO),)]
        copies = [
            remote(last, before, sems, cols, sec_right),
            remote(first, after, sems, cols, sec_left),
        ]
        for copy in copies:
            copy.start()
            sent.append(copy)
        return copies

    def turn_all(read, write):
        def one(y, carry):
            write(y, turned(read(y), nz))
            return carry

        lax.fori_loop(0, ny, one, 0)

    advance(parts)
    loads[2].wait()

    def put_d(y, value):
        d_t[y, PAD : PAD + nx, :] = 6.0 * (value - 1.0)

    turn_all(lambda y: potential_v[y], put_d)
    edges_d = swap_edges(d_t, 1)
    advance(parts)
    loads[1].wait()
    for column in range(2):
        def put_trial(y, value, column=column):
            trial_t[column, y, PAD : PAD + nx, :] = value

        turn_all(lambda y, column=column: trial_v[column, y], put_trial)
        advance(parts)
    edges_trial = swap_edges(trial_t, 2)
    for _ in range(64):
        advance(parts)
    for copy in edges_d + edges_trial:
        copy.wait_recv()

    lanes = lax.broadcasted_iota(jnp.int32, (8, 128), 1)
    inside = lanes < nz

    def field_rows(turn, column, lo, hi):
        def one(block, carry):
            row = pl.multiple_of(block * 8, 8)
            for y in range(ny):
                w[column, y, pl.ds(row, 8), :] = (
                    psi_t[turn, y, pl.ds(row, 8), :] * trial_t[column, y, pl.ds(row, 8), :]
                )
            return carry

        lax.fori_loop(lo, hi, one, 0)

    def step_rows(src, dst, column, scale, sign, lo, hi):
        def one(block, carry):
            row = pl.multiple_of(block * 8, 8)
            for y in range(ny):
                v = stencil(src.at[column], d_t, y, ny, row)
                value = scale * w[column, y, pl.ds(row, 8), :] + sign * v
                dst[column, y, pl.ds(row, 8), :] = jnp.where(inside, value, 0.0)
            return carry

        lax.fori_loop(lo, hi, one, 0)

    def last_rows(turn, column, lo, hi):
        def one(block, carry):
            row = pl.multiple_of(block * 8, 8)
            place = pl.multiple_of(row - PAD, 8)
            for y in range(ny):
                v = stencil(u2.at[column], d_t, y, ny, row)
                value = psi_t[turn, y, pl.ds(row, 8), :] * (
                    0.2 * w[column, y, pl.ds(row, 8), :] + v * (1.0 / 864000.0)
                )
                if turn > 0:
                    value = value + total[column, y, pl.ds(place, 8), :]
                total[column, y, pl.ds(place, 8), :] = value
            return carry

        lax.fori_loop(lo, hi, one, 0)

    a, b = PAD // 8, (PAD + nx) // 8
    for turn in range(ROUNDS):
        def put_psi(y, value, turn=turn):
            psi_t[turn, y, PAD : PAD + nx, :] = value

        def get_psi(y, turn=turn):
            return psi[turn, pl.ds(pl.multiple_of(y * nz, 8), nz), :]

        turn_all(get_psi, put_psi)
        edges = swap_edges(psi_t.at[turn], 1)
        for column in range(2):
            field_rows(turn, column, a, b)
            step_rows(w, u1, column, 72.0, -1.0, a + 1, b - 1)
        for copy in edges:
            copy.wait_recv()
        for column in range(2):
            field_rows(turn, column, a - 1, a)
            field_rows(turn, column, b, b + 1)
            step_rows(w, u1, column, 72.0, -1.0, a - 1, a + 1)
            step_rows(w, u1, column, 72.0, -1.0, b - 1, b + 1)
            step_rows(u1, u2, column, 3600.0, 1.0, a - 1, b + 1)
            last_rows(turn, column, a, b)

    stores = []
    for column in range(2):
        def back(y, carry, column=column):
            out_v[column, y] = total[column, y].T[:nz, :]
            return carry

        lax.fori_loop(0, ny, back, 0)
        store = pltpu.make_async_copy(out_v.at[column], out_ref.at[column], store_sem.at[column])
        store.start()
        stores.append(store)
    for copy in sent:
        copy.wait_send()
    for store in stores:
        store.wait()


def body(trial, orbitals, potential, owner):
    columns, ny, nz, nx = trial.shape
    n_rows = ny * nz
    tall = PAD + nx + PAD
    any_spec = pl.BlockSpec(memory_space=pl.ANY)
    n_sems = 2 * ROUNDS * (2 * (X - 1) + 2 * (Z - 1) + 1) + 2 * (2 + ROUNDS)
    return pl.pallas_call(
        kernel,
        out_shape=jax.ShapeDtypeStruct(trial.shape, F32),
        in_specs=[pl.BlockSpec(memory_space=pltpu.SMEM), any_spec, any_spec, any_spec],
        out_specs=any_spec,
        scratch_shapes=[
            pltpu.VMEM(trial.shape, F32),
            pltpu.VMEM((n_rows, nx), F32),
            pltpu.VMEM((ny, nz, nx), F32),
            pltpu.VMEM((ROUNDS, n_rows, nx), F32),
            pltpu.VMEM((2 * ROUNDS, slot_rows(n_rows // 2), nx), F32),
            pltpu.VMEM((ROUNDS, ny, tall, 128), F32),
            pltpu.VMEM((columns, ny, tall, 128), F32),
            pltpu.VMEM((ny, tall, 128), F32),
            pltpu.VMEM((columns, ny, tall, 128), F32),
            pltpu.VMEM((columns, ny, tall, 128), F32),
            pltpu.VMEM((columns, ny, tall, 128), F32),
            pltpu.VMEM((columns, ny, nx, 128), F32),
            pltpu.VMEM(trial.shape, F32),
            pltpu.SemaphoreType.DMA((3,)),
            pltpu.SemaphoreType.DMA((columns,)),
            pltpu.SemaphoreType.DMA((n_sems,)),
            pltpu.SemaphoreType.DMA((n_sems,)),
        ],
        compiler_params=pltpu.CompilerParams(
            collective_id=0, has_side_effects=True, vmem_limit_bytes=52 * 1024 * 1024
        ),
    )(owner, trial, orbitals.reshape(orbitals.shape[0], n_rows, nx), potential)


def solution(mesh):
    placed = (P("cols", None, None, "sec"), P("cols", None, None, "sec"), P(None, None, "sec"), P())
    return jax.shard_map(
        body, mesh=mesh, in_specs=placed, out_specs=P("cols", None, None, "sec"), check_vma=False
    )
```

```python
import jax
import jax.numpy as jnp
from jax import lax
from jax.experimental import pallas as pl
from jax.experimental.pallas import tpu as pltpu
from jax.sharding import PartitionSpec as P

MESH = pl.DeviceIdType.MESH
F32 = jnp.float32

ROUNDS = 2
X, Z, H = 4, 8, 2
PAD = 16
BLOCK = 16
TOGETHER = ((0, 1),)
HALO = 8


def coords(index):
    return index // (Z * H), (index // H) % Z, index % H


def at(x, z, h):
    return (x * Z + z) * H + h


class Group:
    def __init__(self, name, me):
        self.name, self.me = name, me
        self.size = Z if name == "z" else X * H

    def shifted(self, offset):
        x, z, h = self.me
        if self.name == "z":
            return x, (z + offset) % Z, h
        return (x + offset // H) % X, z, (h + offset % H) % H

    def member(self, offset):
        return at(*self.shifted(offset))

    def place(self, offset=0):
        x, z, h = self.shifted(offset)
        return z if self.name == "z" else x * H + h

    def offset_of(self, root):
        x, z, h = self.me
        rx, rz, rh = root
        if self.name == "z":
            return (z - rz + Z) % Z
        return ((x - rx + X) % X) * H + (h - rh + H) % H


class Sems:
    def __init__(self, send, recv):
        self.send, self.recv, self.count = send, recv, 0

    def take(self):
        self.count += 1
        return self.send.at[self.count - 1], self.recv.at[self.count - 1]


def remote(src, dst, sems, cols, sec):
    send, recv = sems.take()
    return pltpu.make_async_remote_copy(
        src_ref=src, dst_ref=dst, send_sem=send, recv_sem=recv, device_id=(cols, sec), device_id_type=MESH
    )


def rows(ref, start, size):
    return ref.at[pl.ds(pl.multiple_of(start, 8), size), :]


def spread(first_copy, own, base, size, out, landed1, landed2, held, first, second, root, sems, sent):
    sec = lax.axis_index("sec")

    def go(src, dst, cols):
        copy = remote(src, dst, sems, cols, sec)
        copy.start()
        sent.append(copy)
        return copy

    def scatter(src, offset, piece, group, landed):
        return [
            go(rows(src, offset + group.place(k) * piece, piece), landed.at[k], group.member(k))
            for k in range(1, group.size)
        ]

    def taken(copies, src, offset, piece, group, landed):
        landed[0] = rows(src, offset + group.place() * piece, piece)[...]
        for copy in copies:
            copy.wait_recv()
        return landed[group.offset_of(root)]

    def gather(offset, piece, group):
        place = rows(out, offset + group.place() * piece, piece)
        return [go(place, place, group.member(k)) for k in range(1, group.size)]

    piece1 = size // first.size
    piece2 = piece1 // second.size
    inner = base + first.place() * piece1
    copies = scatter(first_copy, base, piece1, first, landed1)
    yield
    held[...] = taken(copies, own, base, piece1, first, landed1)
    copies = scatter(held, 0, piece2, second, landed2)
    yield
    rows(out, inner + second.place() * piece2, piece2)[...] = taken(copies, held, 0, piece2, second, landed2)
    copies = gather(inner, piece2, second)
    yield
    for copy in copies:
        copy.wait_recv()
    copies = gather(base, piece1, first)
    yield
    for copy in copies:
        copy.wait_recv()


def turned(plane, nz):
    return jnp.concatenate([plane, jnp.zeros((128 - nz, 128), F32)], axis=0).T


def along_lanes(fields, band):
    height = fields[0].shape[0]
    whole = jnp.concatenate(fields, axis=0)
    high = whole.astype(jnp.bfloat16)
    low = (whole - high.astype(F32)).astype(jnp.bfloat16)
    both = jnp.concatenate([high, low], axis=1)
    product = jnp.dot(both, band, preferred_element_type=F32)
    return [product[height * i : height * (i + 1), :] for i in range(len(fields))]


def stencil(src, d_ref, band, columns, ny, row, store):
    def read(column, plane, shift):
        return src[column, plane, pl.ds(row + shift, BLOCK), :]

    u = {(c, y): read(c, y, 0) for c in columns for y in range(ny)}
    lanes = dict(zip(u, along_lanes(list(u.values()), band)))
    for c, y in u:
        near = read(c, y, 1) + read(c, y, -1)
        far = read(c, y, 2) + read(c, y, -2)
        for shift in (-1, 1):
            if 0 <= y + shift < ny:
                near = near + u[c, y + shift]
        for shift in (-2, 2):
            if 0 <= y + shift < ny:
                far = far + u[c, y + shift]
        store(c, y, (far - 16.0 * near) + (lanes[c, y] + d_ref[y, pl.ds(row, BLOCK), :] * u[c, y]))


def kernel(
    owner_ref, trial_ref, orbital_ref, potential_ref, out_ref,
    trial_v, orbital_v, potential_v, psi, land_p1, land_p2, land_q1, land_q2, held_p, held_q,
    psi_t, trial_t, d_t, w, u1, u2, total, band_ref,
    load_sem, store_sem, send_sem, recv_sem,
):
    ny, nz, nx = potential_v.shape
    n_rows = ny * nz
    sec = lax.axis_index("sec")
    n_sec = lax.axis_size("sec")
    cols = lax.axis_index("cols")
    me = coords(cols)
    group_xy, group_z = Group("xy", me), Group("z", me)
    sec_right, sec_left = (sec + 1) % n_sec, (sec + n_sec - 1) % n_sec

    barrier = pltpu.get_barrier_semaphore()
    partners = [(g.member(k), sec) for g in (group_xy, group_z) for k in range(1, g.size)]
    partners += [(cols, sec_right), (cols, sec_left)]
    for partner in partners:
        pl.semaphore_signal(barrier, inc=1, device_id=partner, device_id_type=MESH)

    loads = [
        pltpu.make_async_copy(orbital_ref.at[0], orbital_v, load_sem.at[0]),
        pltpu.make_async_copy(potential_ref, potential_v, load_sem.at[1]),
        pltpu.make_async_copy(trial_ref, trial_v, load_sem.at[2]),
    ]
    for load in loads:
        load.start()

    k = lax.broadcasted_iota(jnp.int32, (256, 128), 0) % 128
    n = lax.broadcasted_iota(jnp.int32, (256, 128), 1)
    gap = jnp.abs(k - n)
    weight = jnp.where(gap == 1, -16.0, jnp.where(gap == 2, 1.0, 0.0))
    band_ref[...] = jnp.where((k < nz) & (n < nz), weight, 0.0).astype(jnp.bfloat16)

    pl.semaphore_wait(barrier, len(partners))

    sems = Sems(send_sem, recv_sem)
    sent = []
    size_p = 2 * n_rows // 3
    parts = []
    for turn in range(ROUNDS):
        root = coords(owner_ref[turn])
        parts.append(
            spread(
                orbital_ref.at[0], orbital_v, 0, size_p, psi[turn], land_p1[turn], land_p2[turn],
                held_p[turn], group_xy, group_z, root, sems, sent,
            )
        )
        parts.append(
            spread(
                orbital_ref.at[0], orbital_v, size_p, n_rows - size_p, psi[turn], land_q1[turn],
                land_q2[turn], held_q[turn], group_z, group_xy, root, sems, sent,
            )
        )

    def advance(which):
        for part in which:
            next(part, None)

    def swap_edges(ref, lead):
        every = (slice(None),) * lead
        first = ref.at[every + (pl.ds(PAD, HALO),)]
        last = ref.at[every + (pl.ds(PAD + nx - HALO, HALO),)]
        before = ref.at[every + (pl.ds(PAD - HALO, HALO),)]
        after = ref.at[every + (pl.ds(PAD + nx, HALO),)]
        copies = [
            remote(last, before, sems, cols, sec_right),
            remote(first, after, sems, cols, sec_left),
        ]
        for copy in copies:
            copy.start()
            sent.append(copy)
        return copies

    def turn_all(read, write):
        def one(y, carry):
            write(y, turned(read(y), nz))
            return carry

        lax.fori_loop(0, ny, one, 0)

    advance(parts)
    loads[0].wait()
    loads[1].wait()

    def put_d(y, value):
        d_t[y, PAD : PAD + nx, :] = 6.0 * (value - 1.0)

    turn_all(lambda y: potential_v[y], put_d)
    edges = swap_edges(d_t, 1)
    loads[2].wait()
    for column in range(2):
        def put_trial(y, value, column=column):
            trial_t[column, y, PAD : PAD + nx, :] = value

        turn_all(lambda y, column=column: trial_v[column, y], put_trial)
    edges += swap_edges(trial_t, 2)
    advance(parts)
    advance(parts)
    advance(parts)
    for copy in edges:
        copy.wait_recv()

    def field_rows(turn, lo, hi):
        def one(block, carry):
            row = pl.multiple_of(block * 8, 8)
            for y in range(ny):
                value = psi_t[turn][y, pl.ds(row, 8), :]
                for column in range(2):
                    w[column, y, pl.ds(row, 8), :] = value * trial_t[column, y, pl.ds(row, 8), :]
            return carry

        lax.fori_loop(lo, hi, one, 0)

    def step_rows(src, dst, scale, sign, lo, hi):
        def one(block, carry):
            row = pl.multiple_of(8 * lo + block * BLOCK, 8)
            place = pl.ds(row, BLOCK)

            def store(c, y, v):
                base = scale * w[c, y, place, :]
                dst[c, y, place, :] = base + v if sign > 0 else base - v

            for columns in TOGETHER:
                stencil(src, d_t, band_ref[...], columns, ny, row, store)
            return carry

        lax.fori_loop(0, (hi - lo) * 8 // BLOCK, one, 0)

    def last_rows(turn, columns, lo, hi):
        def one(block, carry):
            row = pl.multiple_of(8 * lo + block * BLOCK, 8)
            place = pl.ds(pl.multiple_of(row - PAD, 8), BLOCK)

            def store(c, y, v):
                here = pl.ds(row, BLOCK)
                value = psi_t[turn][y, here, :] * (0.2 * w[c, y, here, :] + v * (1.0 / 864000.0))
                value = value[:, :nz]
                if turn > 0:
                    value = value + total[c, y, place, :]
                total[c, y, place, :] = value

            stencil(u2, d_t, band_ref[...], columns, ny, row, store)
            return carry

        lax.fori_loop(0, (hi - lo) * 8 // BLOCK, one, 0)

    a, b = PAD // 8, (PAD + nx) // 8
    stores = []
    for turn in range(ROUNDS):
        advance(parts[2 * turn : 2 * turn + 2])

        def put_psi(y, value, turn=turn):
            psi_t[turn][y, PAD : PAD + nx, :] = value

        def get_psi(y, turn=turn):
            return psi[turn][pl.ds(pl.multiple_of(y * nz, 8), nz), :]

        turn_all(get_psi, put_psi)
        edges = swap_edges(psi_t[turn], 1)
        field_rows(turn, a, b)
        step_rows(w, u1, 72.0, -1.0, a + 1, b - 1)
        for copy in edges:
            copy.wait_recv()
        field_rows(turn, a - 1, a)
        field_rows(turn, b, b + 1)
        step_rows(w, u1, 72.0, -1.0, a - 1, a + 1)
        step_rows(w, u1, 72.0, -1.0, b - 1, b + 1)
        step_rows(u1, u2, 3600.0, 1.0, a - 1, b + 1)
        for columns in TOGETHER:
            last_rows(turn, columns, a, b)
            if turn == ROUNDS - 1:
                for c in columns:
                    store = pltpu.make_async_copy(total.at[c], out_ref.at[c], store_sem.at[c])
                    store.start()
                    stores.append(store)

    for copy in sent:
        copy.wait_send()
    for store in stores:
        store.wait()


def body(trial, orbitals, potential, owner):
    columns, ny, nz, nx = trial.shape
    n_rows = ny * nz
    tall = PAD + nx + PAD
    xy = X * H
    size_p, size_q = 2 * n_rows // 3, n_rows // 3
    any_spec = pl.BlockSpec(memory_space=pl.ANY)

    def each_round(*shape):
        return (pltpu.VMEM(shape, F32),) * ROUNDS

    n_sems = 4 * ROUNDS * (xy + Z - 2) + 2 * (2 + ROUNDS)
    out = pl.pallas_call(
        kernel,
        out_shape=jax.ShapeDtypeStruct((columns, ny, nx, nz), F32),
        in_specs=[pl.BlockSpec(memory_space=pltpu.SMEM), any_spec, any_spec, any_spec],
        out_specs=any_spec,
        scratch_shapes=[
            pltpu.VMEM(trial.shape, F32),
            pltpu.VMEM((n_rows, nx), F32),
            pltpu.VMEM((ny, nz, nx), F32),
            each_round(n_rows, nx),
            each_round(xy, size_p // xy, nx),
            each_round(Z, size_p // (xy * Z), nx),
            each_round(Z, size_q // Z, nx),
            each_round(xy, size_q // (xy * Z), nx),
            each_round(size_p // xy, nx),
            each_round(size_q // Z, nx),
            each_round(ny, tall, 128),
            pltpu.VMEM((columns, ny, tall, 128), F32),
            pltpu.VMEM((ny, tall, 128), F32),
            pltpu.VMEM((columns, ny, tall, 128), F32),
            pltpu.VMEM((columns, ny, tall, 128), F32),
            pltpu.VMEM((columns, ny, tall, 128), F32),
            pltpu.VMEM((columns, ny, nx, nz), F32),
            pltpu.VMEM((256, 128), jnp.bfloat16),
            pltpu.SemaphoreType.DMA((3,)),
            pltpu.SemaphoreType.DMA((columns,)),
            pltpu.SemaphoreType.DMA((n_sems,)),
            pltpu.SemaphoreType.DMA((n_sems,)),
        ],
        compiler_params=pltpu.CompilerParams(
            collective_id=0, has_side_effects=True, vmem_limit_bytes=60 * 1024 * 1024
        ),
    )(owner, trial, orbitals.reshape(orbitals.shape[0], n_rows, nx), potential)
    return out.transpose(0, 1, 3, 2)


def solution(mesh):
    placed = (P("cols", None, None, "sec"), P("cols", None, None, "sec"), P(None, None, "sec"), P())
    return jax.shard_map(
        body, mesh=mesh, in_specs=placed, out_specs=P("cols", None, None, "sec"), check_vma=False
    )
```

```python
import jax
import jax.numpy as jnp
from jax import lax
from jax.experimental import pallas as pl
from jax.experimental.pallas import tpu as pltpu
from jax.sharding import PartitionSpec as P

MESH = pl.DeviceIdType.MESH
F32 = jnp.float32

ROUNDS = 2
X, Z, H = 4, 8, 2
PAD = 16
BLOCK = 16
HALO = 8


def coords(index):
    return index // (Z * H), (index // H) % Z, index % H


def at(x, z, h):
    return (x * Z + z) * H + h


class Group:
    def __init__(self, name, me):
        self.name, self.me = name, me
        self.size = Z if name == "z" else X * H

    def shifted(self, offset):
        x, z, h = self.me
        if self.name == "z":
            return x, (z + offset) % Z, h
        return (x + offset // H) % X, z, (h + offset % H) % H

    def member(self, offset):
        return at(*self.shifted(offset))

    def place(self, offset=0):
        x, z, h = self.shifted(offset)
        return z if self.name == "z" else x * H + h

    def offset_of(self, root):
        x, z, h = self.me
        rx, rz, rh = root
        if self.name == "z":
            return (z - rz + Z) % Z
        return ((x - rx + X) % X) * H + (h - rh + H) % H


class Sems:
    def __init__(self, send, recv):
        self.send, self.recv, self.count = send, recv, 0

    def take(self):
        self.count += 1
        return self.send.at[self.count - 1], self.recv.at[self.count - 1]


def remote(src, dst, sems, cols, sec):
    send, recv = sems.take()
    return pltpu.make_async_remote_copy(
        src_ref=src, dst_ref=dst, send_sem=send, recv_sem=recv, device_id=(cols, sec), device_id_type=MESH
    )


def rows(ref, start, size):
    return ref.at[pl.ds(pl.multiple_of(start, 8), size), :]


def spread(first_copy, own, base, size, out, landed1, landed2, held, first, second, root, sems, sent):
    sec = lax.axis_index("sec")

    def go(src, dst, cols):
        copy = remote(src, dst, sems, cols, sec)
        copy.start()
        return copy

    def scatter(src, offset, piece, group, landed):
        return [
            go(rows(src, offset + group.place(k) * piece, piece), landed.at[k], group.member(k))
            for k in range(1, group.size)
        ]

    def taken(copies, src, offset, piece, group, landed):
        landed[0] = rows(src, offset + group.place() * piece, piece)[...]
        for copy in copies:
            copy.wait_recv()
        return landed[group.offset_of(root)]

    def gather(offset, piece, group):
        place = rows(out, offset + group.place() * piece, piece)
        return [go(place, place, group.member(k)) for k in range(1, group.size)]

    piece1 = size // first.size
    piece2 = piece1 // second.size
    inner = base + first.place() * piece1
    copies = scatter(first_copy, base, piece1, first, landed1)
    yield copies
    held[...] = taken(copies, own, base, piece1, first, landed1)
    copies = scatter(held, 0, piece2, second, landed2)
    sent += copies
    yield
    rows(out, inner + second.place() * piece2, piece2)[...] = taken(copies, held, 0, piece2, second, landed2)
    copies = gather(inner, piece2, second)
    sent += copies
    yield
    for copy in copies:
        copy.wait_recv()
    copies = gather(base, piece1, first)
    yield copies
    for copy in copies:
        copy.wait_recv()


def turned(plane, nz):
    return jnp.concatenate([plane, jnp.zeros((128 - nz, 128), F32)], axis=0).T


def along_lanes(fields, band):
    height = fields[0].shape[0]
    whole = jnp.concatenate(fields, axis=0)
    high = whole.astype(jnp.bfloat16)
    low = (whole - high.astype(F32)).astype(jnp.bfloat16)
    both = jnp.concatenate([high, low], axis=1)
    product = jnp.dot(both, band, preferred_element_type=F32)
    return [product[height * i : height * (i + 1), :] for i in range(len(fields))]


def stencil(src, d_ref, band, columns, ny, row, store):
    def read(column, plane, shift):
        return src[column, plane, pl.ds(row + shift, BLOCK), :]

    u = {(c, y): read(c, y, 0) for c in columns for y in range(ny)}
    lanes = dict(zip(u, along_lanes(list(u.values()), band)))
    for c, y in u:
        near = read(c, y, 1) + read(c, y, -1)
        far = read(c, y, 2) + read(c, y, -2)
        for shift in (-1, 1):
            if 0 <= y + shift < ny:
                near = near + u[c, y + shift]
        for shift in (-2, 2):
            if 0 <= y + shift < ny:
                far = far + u[c, y + shift]
        store(c, y, (far - 16.0 * near) + (lanes[c, y] + d_ref[y, pl.ds(row, BLOCK), :] * u[c, y]))


def kernel(
    owner_ref, trial_ref, orbital_ref, potential_ref, out_ref,
    trial_v, orbital_v, potential_v, psi, land_p1, land_p2, land_q1, land_q2, held_p, held_q,
    psi_t, trial_t, d_t, w, u1, u2, total, band_ref,
    load_sem, store_sem, send_sem, recv_sem,
):
    ny, nz, nx = potential_v.shape
    n_rows = ny * nz
    sec = lax.axis_index("sec")
    n_sec = lax.axis_size("sec")
    cols = lax.axis_index("cols")
    me = coords(cols)
    group_xy, group_z = Group("xy", me), Group("z", me)
    sec_right, sec_left = (sec + 1) % n_sec, (sec + n_sec - 1) % n_sec

    barrier = pltpu.get_barrier_semaphore()
    partners = [(g.member(k), sec) for g in (group_xy, group_z) for k in range(1, g.size)]
    partners += [(cols, sec_right), (cols, sec_left)]
    for partner in partners:
        pl.semaphore_signal(barrier, inc=1, device_id=partner, device_id_type=MESH)

    loads = [
        pltpu.make_async_copy(orbital_ref.at[0], orbital_v, load_sem.at[0]),
        pltpu.make_async_copy(potential_ref, potential_v, load_sem.at[1]),
        pltpu.make_async_copy(trial_ref, trial_v, load_sem.at[2]),
    ]
    for load in loads:
        load.start()

    k = lax.broadcasted_iota(jnp.int32, (256, 128), 0) % 128
    n = lax.broadcasted_iota(jnp.int32, (256, 128), 1)
    gap = jnp.abs(k - n)
    weight = jnp.where(gap == 1, -16.0, jnp.where(gap == 2, 1.0, 0.0))
    band_ref[...] = jnp.where((k < nz) & (n < nz), weight, 0.0).astype(jnp.bfloat16)

    pl.semaphore_wait(barrier, len(partners))

    sems = Sems(send_sem, recv_sem)
    sent = []
    size_p = 2 * n_rows // 3
    parts = []
    for turn in range(ROUNDS):
        root = coords(owner_ref[turn])
        parts.append(
            spread(
                orbital_ref.at[0], orbital_v, 0, size_p, psi[turn], land_p1[turn], land_p2[turn],
                held_p[turn], group_xy, group_z, root, sems, sent,
            )
        )
        parts.append(
            spread(
                orbital_ref.at[0], orbital_v, size_p, n_rows - size_p, psi[turn], land_q1[turn],
                land_q2[turn], held_q[turn], group_z, group_xy, root, sems, sent,
            )
        )

    def advance(turn):
        return [copy for part in parts[2 * turn : 2 * turn + 2] for copy in next(part, None) or ()]

    def swap_edges(ref, lead):
        every = (slice(None),) * lead
        first = ref.at[every + (pl.ds(PAD, HALO),)]
        last = ref.at[every + (pl.ds(PAD + nx - HALO, HALO),)]
        before = ref.at[every + (pl.ds(PAD - HALO, HALO),)]
        after = ref.at[every + (pl.ds(PAD + nx, HALO),)]
        copies = [
            remote(last, before, sems, cols, sec_right),
            remote(first, after, sems, cols, sec_left),
        ]
        for copy in copies:
            copy.start()
            sent.append(copy)
        return copies

    def turn_all(read, write):
        def one(y, carry):
            write(y, turned(read(y), nz))
            return carry

        lax.fori_loop(0, ny, one, 0)

    def put_d(y, value):
        d_t[y, PAD : PAD + nx, :] = 6.0 * (value - 1.0)

    sent += advance(0) + advance(1)
    loads[1].wait()
    turn_all(lambda y: potential_v[y], put_d)
    edges_in = swap_edges(d_t, 1)
    loads[2].wait()
    for column in range(2):
        def put_trial(y, value, column=column):
            trial_t[column, y, PAD : PAD + nx, :] = value

        turn_all(lambda y, column=column: trial_v[column, y], put_trial)
    edges_in += swap_edges(trial_t, 2)
    loads[0].wait()
    for turn in (0, 1, 0, 1):
        advance(turn)
    ahead = advance(0)
    for copy in edges_in:
        copy.wait_recv()
    for copy in ahead:
        copy.wait_send()
    sent += advance(1)

    def field_rows(turn, lo, hi):
        def one(block, carry):
            row = pl.multiple_of(block * 8, 8)
            for y in range(ny):
                value = psi_t[turn][y, pl.ds(row, 8), :]
                for column in range(2):
                    w[column, y, pl.ds(row, 8), :] = value * trial_t[column, y, pl.ds(row, 8), :]
            return carry

        lax.fori_loop(lo, hi, one, 0)

    def step_rows(src, dst, scale, sign, lo, hi):
        def one(block, carry):
            row = pl.multiple_of(8 * lo + block * BLOCK, 8)
            place = pl.ds(row, BLOCK)

            def store(c, y, v):
                base = scale * w[c, y, place, :]
                dst[c, y, place, :] = base + v if sign > 0 else base - v

            stencil(src, d_t, band_ref[...], (0, 1), ny, row, store)
            return carry

        lax.fori_loop(0, (hi - lo) * 8 // BLOCK, one, 0)

    def last_rows(turn, columns, lo, hi):
        def one(block, carry):
            row = pl.multiple_of(8 * lo + block * BLOCK, 8)
            place = pl.ds(pl.multiple_of(row - PAD, 8), BLOCK)

            def store(c, y, v):
                here = pl.ds(row, BLOCK)
                value = psi_t[turn][y, here, :] * (0.2 * w[c, y, here, :] + v * (1.0 / 864000.0))
                value = value[:, :nz]
                if turn > 0:
                    value = value + total[c, y, place, :]
                total[c, y, place, :] = value

            stencil(u2, d_t, band_ref[...], columns, ny, row, store)
            return carry

        lax.fori_loop(0, (hi - lo) * 8 // BLOCK, one, 0)

    a, b = PAD // 8, (PAD + nx) // 8

    def arrive(turn):
        def put_psi(y, value):
            psi_t[turn][y, PAD : PAD + nx, :] = value

        def get_psi(y):
            return psi[turn][pl.ds(pl.multiple_of(y * nz, 8), nz), :]

        advance(turn)
        turn_all(get_psi, put_psi)
        return swap_edges(psi_t[turn], 1)

    def first_two(turn, edges):
        field_rows(turn, a, b)
        step_rows(w, u1, 72.0, -1.0, a + 1, b - 1)
        for copy in edges:
            copy.wait_recv()
        field_rows(turn, a - 1, a)
        field_rows(turn, b, b + 1)
        step_rows(w, u1, 72.0, -1.0, a - 1, a + 1)
        step_rows(w, u1, 72.0, -1.0, b - 1, b + 1)
        step_rows(u1, u2, 3600.0, 1.0, a - 1, b + 1)

    first_two(0, arrive(0))
    edges = arrive(1)
    last_rows(0, (0, 1), a, b)
    first_two(1, edges)
    stores = []
    for c in range(2):
        last_rows(1, (c,), a, b)
        store = pltpu.make_async_copy(total.at[c], out_ref.at[c], store_sem.at[c])
        store.start()
        stores.append(store)

    for copy in sent:
        copy.wait_send()
    for store in stores:
        store.wait()


def body(trial, orbitals, potential, owner):
    columns, ny, nz, nx = trial.shape
    n_rows = ny * nz
    tall = PAD + nx + PAD
    xy = X * H
    size_p, size_q = 2 * n_rows // 3, n_rows // 3
    any_spec = pl.BlockSpec(memory_space=pl.ANY)

    def each_round(*shape):
        return (pltpu.VMEM(shape, F32),) * ROUNDS

    n_sems = 4 * ROUNDS * (xy + Z - 2) + 2 * (2 + ROUNDS)
    out = pl.pallas_call(
        kernel,
        out_shape=jax.ShapeDtypeStruct((columns, ny, nx, nz), F32),
        in_specs=[pl.BlockSpec(memory_space=pltpu.SMEM), any_spec, any_spec, any_spec],
        out_specs=any_spec,
        scratch_shapes=[
            pltpu.VMEM(trial.shape, F32),
            pltpu.VMEM((n_rows, nx), F32),
            pltpu.VMEM((ny, nz, nx), F32),
            each_round(n_rows, nx),
            each_round(xy, size_p // xy, nx),
            each_round(Z, size_p // (xy * Z), nx),
            each_round(Z, size_q // Z, nx),
            each_round(xy, size_q // (xy * Z), nx),
            each_round(size_p // xy, nx),
            each_round(size_q // Z, nx),
            each_round(ny, tall, 128),
            pltpu.VMEM((columns, ny, tall, 128), F32),
            pltpu.VMEM((ny, tall, 128), F32),
            pltpu.VMEM((columns, ny, tall, 128), F32),
            pltpu.VMEM((columns, ny, tall, 128), F32),
            pltpu.VMEM((columns, ny, tall, 128), F32),
            pltpu.VMEM((columns, ny, nx, nz), F32),
            pltpu.VMEM((256, 128), jnp.bfloat16),
            pltpu.SemaphoreType.DMA((3,)),
            pltpu.SemaphoreType.DMA((columns,)),
            pltpu.SemaphoreType.DMA((n_sems,)),
            pltpu.SemaphoreType.DMA((n_sems,)),
        ],
        compiler_params=pltpu.CompilerParams(
            collective_id=0, has_side_effects=True, vmem_limit_bytes=60 * 1024 * 1024
        ),
    )(owner, trial, orbitals.reshape(orbitals.shape[0], n_rows, nx), potential)
    return out.transpose(0, 1, 3, 2)


def solution(mesh):
    placed = (P("cols", None, None, "sec"), P("cols", None, None, "sec"), P(None, None, "sec"), P())
    return jax.shard_map(
        body, mesh=mesh, in_specs=placed, out_specs=P("cols", None, None, "sec"), check_vma=False
    )
```

```python
import jax
import jax.numpy as jnp
from jax import lax
from jax.experimental import pallas as pl
from jax.experimental.pallas import tpu as pltpu
from jax.sharding import PartitionSpec as P

MESH = pl.DeviceIdType.MESH
F32 = jnp.float32

ROUNDS = 2
X, Z, H = 4, 8, 2
PAD = 16
PARTS = 4
BLOCK = 16
HALO = 8


def coords(index):
    return index // (Z * H), (index // H) % Z, index % H


def at(x, z, h):
    return (x * Z + z) * H + h


class Group:
    def __init__(self, name, me):
        self.name, self.me = name, me
        self.size = Z if name == "z" else X * H

    def shifted(self, offset):
        x, z, h = self.me
        if self.name == "z":
            return x, (z + offset) % Z, h
        return (x + offset // H) % X, z, (h + offset % H) % H

    def member(self, offset):
        return at(*self.shifted(offset))

    def place(self, offset=0):
        x, z, h = self.shifted(offset)
        return z if self.name == "z" else x * H + h

    def offset_of(self, root):
        x, z, h = self.me
        rx, rz, rh = root
        if self.name == "z":
            return (z - rz + Z) % Z
        return ((x - rx + X) % X) * H + (h - rh + H) % H


class Sems:
    def __init__(self, send, recv):
        self.send, self.recv, self.count = send, recv, 0

    def take(self):
        self.count += 1
        return self.send.at[self.count - 1], self.recv.at[self.count - 1]


def remote(src, dst, sems, cols, sec):
    send, recv = sems.take()
    return pltpu.make_async_remote_copy(
        src_ref=src, dst_ref=dst, send_sem=send, recv_sem=recv, device_id=(cols, sec), device_id_type=MESH
    )


def rows(ref, start, size):
    return ref.at[pl.ds(pl.multiple_of(start, 8), size), :]


def spread(first_copy, own, base, size, out, landed1, landed2, held, first, second, root, sems, sent):
    sec = lax.axis_index("sec")

    def go(src, dst, cols):
        copy = remote(src, dst, sems, cols, sec)
        copy.start()
        return copy

    def scatter(src, offset, piece, group, landed):
        return [
            go(rows(src, offset + group.place(k) * piece, piece), landed.at[k], group.member(k))
            for k in range(1, group.size)
        ]

    def taken(copies, src, offset, piece, group, landed):
        landed[0] = rows(src, offset + group.place() * piece, piece)[...]
        for copy in copies:
            copy.wait_recv()
        return landed[group.offset_of(root)]

    def gather(offset, piece, group):
        place = rows(out, offset + group.place() * piece, piece)
        return [go(place, place, group.member(k)) for k in range(1, group.size)]

    piece1 = size // first.size
    piece2 = piece1 // second.size
    inner = base + first.place() * piece1
    copies = scatter(first_copy, base, piece1, first, landed1)
    yield copies
    held[...] = taken(copies, own, base, piece1, first, landed1)
    copies = scatter(held, 0, piece2, second, landed2)
    sent += copies
    yield
    rows(out, inner + second.place() * piece2, piece2)[...] = taken(copies, held, 0, piece2, second, landed2)
    copies = gather(inner, piece2, second)
    sent += copies
    yield
    for copy in copies:
        copy.wait_recv()
    copies = gather(base, piece1, first)
    yield copies
    for copy in copies:
        copy.wait_recv()


def turned(plane, nz):
    return jnp.concatenate([plane, jnp.zeros((128 - nz, 128), F32)], axis=0).T


def along_lanes(fields, band):
    height = fields[0].shape[0]
    whole = jnp.concatenate(fields, axis=0)
    high = whole.astype(jnp.bfloat16)
    low = (whole - high.astype(F32)).astype(jnp.bfloat16)
    both = jnp.concatenate([high, low], axis=1)
    product = jnp.dot(both, band, preferred_element_type=F32)
    return [product[height * i : height * (i + 1), :] for i in range(len(fields))]


def stencil(src, d_ref, band, columns, ny, row, store):
    def read(column, plane, shift):
        return src[column, plane, pl.ds(row + shift, BLOCK), :]

    u = {(c, y): read(c, y, 0) for c in columns for y in range(ny)}
    lanes = dict(zip(u, along_lanes(list(u.values()), band)))
    for c, y in u:
        near = read(c, y, 1) + read(c, y, -1)
        far = read(c, y, 2) + read(c, y, -2)
        for shift in (-1, 1):
            if 0 <= y + shift < ny:
                near = near + u[c, y + shift]
        for shift in (-2, 2):
            if 0 <= y + shift < ny:
                far = far + u[c, y + shift]
        store(c, y, (far - 16.0 * near) + (lanes[c, y] + d_ref[y, pl.ds(row, BLOCK), :] * u[c, y]))


def kernel(
    owner_ref, trial_ref, orbital_ref, potential_ref, out_ref,
    trial_v, orbital_v, potential_v, psi, land_p1, land_p2, land_q1, land_q2, held_p, held_q,
    psi_t, trial_t, d_t, w, u1, u2, total, band_ref,
    load_sem, store_sem, send_sem, recv_sem,
):
    ny, nz, nx = potential_v.shape
    n_rows = ny * nz
    sec = lax.axis_index("sec")
    n_sec = lax.axis_size("sec")
    cols = lax.axis_index("cols")
    me = coords(cols)
    group_xy, group_z = Group("xy", me), Group("z", me)
    sec_right, sec_left = (sec + 1) % n_sec, (sec + n_sec - 1) % n_sec

    barrier = pltpu.get_barrier_semaphore()
    partners = [(g.member(k), sec) for g in (group_xy, group_z) for k in range(1, g.size)]
    partners += [(cols, sec_right), (cols, sec_left)]
    for partner in partners:
        pl.semaphore_signal(barrier, inc=1, device_id=partner, device_id_type=MESH)

    loads = [
        pltpu.make_async_copy(orbital_ref.at[0], orbital_v, load_sem.at[0]),
        pltpu.make_async_copy(potential_ref, potential_v, load_sem.at[1]),
        pltpu.make_async_copy(trial_ref, trial_v, load_sem.at[2]),
    ]
    for load in loads:
        load.start()

    k = lax.broadcasted_iota(jnp.int32, (256, 128), 0) % 128
    n = lax.broadcasted_iota(jnp.int32, (256, 128), 1)
    gap = jnp.abs(k - n)
    weight = jnp.where(gap == 1, -16.0, jnp.where(gap == 2, 1.0, 0.0))
    band_ref[...] = jnp.where((k < nz) & (n < nz), weight, 0.0).astype(jnp.bfloat16)

    pl.semaphore_wait(barrier, len(partners))

    sems = Sems(send_sem, recv_sem)
    sent = []
    size_p = 2 * n_rows // 3
    parts = []
    for turn in range(ROUNDS):
        root = coords(owner_ref[turn])
        parts.append(
            spread(
                orbital_ref.at[0], orbital_v, 0, size_p, psi[turn], land_p1[turn], land_p2[turn],
                held_p[turn], group_xy, group_z, root, sems, sent,
            )
        )
        parts.append(
            spread(
                orbital_ref.at[0], orbital_v, size_p, n_rows - size_p, psi[turn], land_q1[turn],
                land_q2[turn], held_q[turn], group_z, group_xy, root, sems, sent,
            )
        )

    def advance(turn):
        return [copy for part in parts[2 * turn : 2 * turn + 2] for copy in next(part, None) or ()]

    def swap_edges(ref, lead):
        every = (slice(None),) * lead
        first = ref.at[every + (pl.ds(PAD, HALO),)]
        last = ref.at[every + (pl.ds(PAD + nx - HALO, HALO),)]
        before = ref.at[every + (pl.ds(PAD - HALO, HALO),)]
        after = ref.at[every + (pl.ds(PAD + nx, HALO),)]
        copies = [
            remote(last, before, sems, cols, sec_right),
            remote(first, after, sems, cols, sec_left),
        ]
        for copy in copies:
            copy.start()
            sent.append(copy)
        return copies

    def turn_all(read, write):
        def one(y, carry):
            write(y, turned(read(y), nz))
            return carry

        lax.fori_loop(0, ny, one, 0, unroll=4)

    def put_d(y, value):
        d_t[y, PAD : PAD + nx, :] = 6.0 * (value - 1.0)

    sent += advance(0) + advance(1)
    loads[1].wait()
    turn_all(lambda y: potential_v[y], put_d)
    edges_in = swap_edges(d_t, 1)
    loads[2].wait()
    for column in range(2):
        def put_trial(y, value, column=column):
            trial_t[column, y, PAD : PAD + nx, :] = value

        turn_all(lambda y, column=column: trial_v[column, y], put_trial)
    edges_in += swap_edges(trial_t, 2)
    loads[0].wait()
    for turn in (0, 1, 0, 1):
        advance(turn)
    ahead = advance(0)
    for copy in edges_in:
        copy.wait_recv()
    for copy in ahead:
        copy.wait_send()
    sent += advance(1)

    def field_rows(turn, lo, hi):
        def one(block, carry):
            row = pl.multiple_of(block * 8, 8)
            for y in range(ny):
                value = psi_t[turn][y, pl.ds(row, 8), :]
                for column in range(2):
                    w[column, y, pl.ds(row, 8), :] = value * trial_t[column, y, pl.ds(row, 8), :]
            return carry

        lax.fori_loop(lo, hi, one, 0)

    def step_rows(src, dst, scale, sign, lo, hi):
        def one(block, carry):
            row = pl.multiple_of(8 * lo + block * BLOCK, 8)
            place = pl.ds(row, BLOCK)

            def store(c, y, v):
                base = scale * w[c, y, place, :]
                dst[c, y, place, :] = base + v if sign > 0 else base - v

            stencil(src, d_t, band_ref[...], (0, 1), ny, row, store)
            return carry

        lax.fori_loop(0, (hi - lo) * 8 // BLOCK, one, 0)

    def last_rows(turn, columns, lo, hi):
        def one(block, carry):
            row = pl.multiple_of(8 * lo + block * BLOCK, 8)
            place = pl.ds(pl.multiple_of(row - PAD, 8), BLOCK)

            def store(c, y, v):
                here = pl.ds(row, BLOCK)
                value = psi_t[turn][y, here, :] * (0.2 * w[c, y, here, :] + v * (1.0 / 864000.0))
                value = value[:, :nz]
                if turn > 0:
                    value = value + total[c, y, place, :]
                total[c, y, place, :] = value

            stencil(u2, d_t, band_ref[...], columns, ny, row, store)
            return carry

        lax.fori_loop(0, (hi - lo) * 8 // BLOCK, one, 0)

    a, b = PAD // 8, (PAD + nx) // 8

    def arrive(turn):
        def put_psi(y, value):
            psi_t[turn][y, PAD : PAD + nx, :] = value

        def get_psi(y):
            return psi[turn][pl.ds(pl.multiple_of(y * nz, 8), nz), :]

        advance(turn)
        turn_all(get_psi, put_psi)
        return swap_edges(psi_t[turn], 1)

    def first_two(turn, edges):
        field_rows(turn, a, b)
        step_rows(w, u1, 72.0, -1.0, a + 1, b - 1)
        for copy in edges:
            copy.wait_recv()
        field_rows(turn, a - 1, a)
        field_rows(turn, b, b + 1)
        step_rows(w, u1, 72.0, -1.0, a - 1, a + 1)
        step_rows(w, u1, 72.0, -1.0, b - 1, b + 1)
        step_rows(u1, u2, 3600.0, 1.0, a - 1, b + 1)

    first_two(0, arrive(0))
    edges = arrive(1)
    last_rows(0, (0, 1), a, b)
    first_two(1, edges)
    stores = []
    for part in range(PARTS):
        tall = nx // PARTS
        last_rows(1, (0, 1), a + part * tall // 8, a + (part + 1) * tall // 8)
        window = (slice(None), slice(None), pl.ds(part * tall, tall))
        store = pltpu.make_async_copy(total.at[window], out_ref.at[window], store_sem.at[part])
        store.start()
        stores.append(store)

    for copy in sent:
        copy.wait_send()
    for store in stores:
        store.wait()


def body(trial, orbitals, potential, owner):
    columns, ny, nz, nx = trial.shape
    n_rows = ny * nz
    tall = PAD + nx + PAD
    xy = X * H
    size_p, size_q = 2 * n_rows // 3, n_rows // 3
    any_spec = pl.BlockSpec(memory_space=pl.ANY)

    def each_round(*shape):
        return (pltpu.VMEM(shape, F32),) * ROUNDS

    n_sems = 4 * ROUNDS * (xy + Z - 2) + 2 * (2 + ROUNDS)
    out = pl.pallas_call(
        kernel,
        out_shape=jax.ShapeDtypeStruct((columns, ny, nx, nz), F32),
        in_specs=[pl.BlockSpec(memory_space=pltpu.SMEM), any_spec, any_spec, any_spec],
        out_specs=any_spec,
        scratch_shapes=[
            pltpu.VMEM(trial.shape, F32),
            pltpu.VMEM((n_rows, nx), F32),
            pltpu.VMEM((ny, nz, nx), F32),
            each_round(n_rows, nx),
            each_round(xy, size_p // xy, nx),
            each_round(Z, size_p // (xy * Z), nx),
            each_round(Z, size_q // Z, nx),
            each_round(xy, size_q // (xy * Z), nx),
            each_round(size_p // xy, nx),
            each_round(size_q // Z, nx),
            each_round(ny, tall, 128),
            pltpu.VMEM((columns, ny, tall, 128), F32),
            pltpu.VMEM((ny, tall, 128), F32),
            pltpu.VMEM((columns, ny, tall, 128), F32),
            pltpu.VMEM((columns, ny, tall, 128), F32),
            pltpu.VMEM((columns, ny, tall, 128), F32),
            pltpu.VMEM((columns, ny, nx, nz), F32),
            pltpu.VMEM((256, 128), jnp.bfloat16),
            pltpu.SemaphoreType.DMA((3,)),
            pltpu.SemaphoreType.DMA((PARTS,)),
            pltpu.SemaphoreType.DMA((n_sems,)),
            pltpu.SemaphoreType.DMA((n_sems,)),
        ],
        compiler_params=pltpu.CompilerParams(
            collective_id=0, has_side_effects=True, vmem_limit_bytes=60 * 1024 * 1024
        ),
    )(owner, trial, orbitals.reshape(orbitals.shape[0], n_rows, nx), potential)
    return out.transpose(0, 1, 3, 2)


def solution(mesh):
    placed = (P("cols", None, None, "sec"), P("cols", None, None, "sec"), P(None, None, "sec"), P())
    return jax.shard_map(
        body, mesh=mesh, in_specs=placed, out_specs=P("cols", None, None, "sec"), check_vma=False
    )
```

```python
import jax
import jax.numpy as jnp
from jax import lax
from jax.experimental import pallas as pl
from jax.experimental.pallas import tpu as pltpu
from jax.sharding import PartitionSpec as P

MESH = pl.DeviceIdType.MESH
F32 = jnp.float32

ROUNDS = 2
X, Z, H = 4, 8, 2
PAD = 16
PARTS = 4
BLOCK = 16
HALO = 8


def coords(index):
    return index // (Z * H), (index // H) % Z, index % H


def at(x, z, h):
    return (x * Z + z) * H + h


class Group:
    def __init__(self, name, me):
        self.name, self.me = name, me
        self.size = Z if name == "z" else X * H

    def shifted(self, offset):
        x, z, h = self.me
        if self.name == "z":
            return x, (z + offset) % Z, h
        return (x + offset // H) % X, z, (h + offset % H) % H

    def member(self, offset):
        return at(*self.shifted(offset))

    def place(self, offset=0):
        x, z, h = self.shifted(offset)
        return z if self.name == "z" else x * H + h

    def offset_of(self, root):
        x, z, h = self.me
        rx, rz, rh = root
        if self.name == "z":
            return (z - rz + Z) % Z
        return ((x - rx + X) % X) * H + (h - rh + H) % H


class Sems:
    def __init__(self, send, recv):
        self.send, self.recv, self.count = send, recv, 0

    def take(self):
        self.count += 1
        return self.send.at[self.count - 1], self.recv.at[self.count - 1]


def remote(src, dst, sems, cols, sec):
    send, recv = sems.take()
    return pltpu.make_async_remote_copy(
        src_ref=src, dst_ref=dst, send_sem=send, recv_sem=recv, device_id=(cols, sec), device_id_type=MESH
    )


def rows(ref, start, size):
    return ref.at[pl.ds(pl.multiple_of(start, 8), size), :]


def spread(first_copy, own, base, size, out, landed1, landed2, held, first, second, root, sems, sent):
    sec = lax.axis_index("sec")

    def go(src, dst, cols):
        copy = remote(src, dst, sems, cols, sec)
        copy.start()
        return copy

    def scatter(src, offset, piece, group, landed):
        return [
            go(rows(src, offset + group.place(k) * piece, piece), landed.at[k], group.member(k))
            for k in range(1, group.size)
        ]

    def taken(copies, src, offset, piece, group, landed):
        landed[0] = rows(src, offset + group.place() * piece, piece)[...]
        for copy in copies:
            copy.wait_recv()
        return landed[group.offset_of(root)]

    def gather(offset, piece, group):
        place = rows(out, offset + group.place() * piece, piece)
        return [go(place, place, group.member(k)) for k in range(1, group.size)]

    piece1 = size // first.size
    piece2 = piece1 // second.size
    inner = base + first.place() * piece1
    copies = scatter(first_copy, base, piece1, first, landed1)
    yield copies
    held[...] = taken(copies, own, base, piece1, first, landed1)
    copies = scatter(held, 0, piece2, second, landed2)
    sent += copies
    yield
    rows(out, inner + second.place() * piece2, piece2)[...] = taken(copies, held, 0, piece2, second, landed2)
    copies = gather(inner, piece2, second)
    sent += copies
    yield
    for copy in copies:
        copy.wait_recv()
    copies = gather(base, piece1, first)
    yield copies
    for copy in copies:
        copy.wait_recv()


def turned(plane, nz):
    return jnp.concatenate([plane, jnp.zeros((128 - nz, 128), F32)], axis=0).T


def along_lanes(fields, band):
    height = fields[0].shape[0]
    whole = jnp.concatenate(fields, axis=0)
    high = whole.astype(jnp.bfloat16)
    low = (whole - high.astype(F32)).astype(jnp.bfloat16)
    both = jnp.concatenate([high, low], axis=1)
    product = jnp.dot(both, band, preferred_element_type=F32)
    return [product[height * i : height * (i + 1), :] for i in range(len(fields))]


def stencil(src, d_ref, band, columns, ny, row, store):
    def read(column, plane, shift):
        return src[column, plane, pl.ds(row + shift, BLOCK), :]

    u = {(c, y): read(c, y, 0) for c in columns for y in range(ny)}
    lanes = dict(zip(u, along_lanes(list(u.values()), band)))
    for c, y in u:
        near = read(c, y, 1) + read(c, y, -1)
        far = read(c, y, 2) + read(c, y, -2)
        for shift in (-1, 1):
            if 0 <= y + shift < ny:
                near = near + u[c, y + shift]
        for shift in (-2, 2):
            if 0 <= y + shift < ny:
                far = far + u[c, y + shift]
        store(c, y, (far - 16.0 * near) + (lanes[c, y] + d_ref[y, pl.ds(row, BLOCK), :] * u[c, y]))


def kernel(
    owner_ref, trial_ref, orbital_ref, potential_ref, out_ref,
    trial_v, orbital_v, potential_v, psi, land_p1, land_p2, land_q1, land_q2, held_p, held_q,
    psi_t, trial_t, d_t, w, u1, u2, total, band_ref,
    load_sem, store_sem, send_sem, recv_sem,
):
    ny, nz, nx = potential_v.shape
    n_rows = ny * nz
    sec = lax.axis_index("sec")
    n_sec = lax.axis_size("sec")
    cols = lax.axis_index("cols")
    me = coords(cols)
    group_xy, group_z = Group("xy", me), Group("z", me)
    sec_right, sec_left = (sec + 1) % n_sec, (sec + n_sec - 1) % n_sec

    barrier = pltpu.get_barrier_semaphore()
    partners = [(g.member(k), sec) for g in (group_xy, group_z) for k in range(1, g.size)]
    partners += [(cols, sec_right), (cols, sec_left)]
    for partner in partners:
        pl.semaphore_signal(barrier, inc=1, device_id=partner, device_id_type=MESH)

    loads = [
        pltpu.make_async_copy(orbital_ref.at[0], orbital_v, load_sem.at[0]),
        pltpu.make_async_copy(potential_ref, potential_v, load_sem.at[1]),
        pltpu.make_async_copy(trial_ref, trial_v, load_sem.at[2]),
    ]
    for load in loads:
        load.start()

    k = lax.broadcasted_iota(jnp.int32, (256, 128), 0) % 128
    n = lax.broadcasted_iota(jnp.int32, (256, 128), 1)
    gap = jnp.abs(k - n)
    weight = jnp.where(gap == 1, -16.0, jnp.where(gap == 2, 1.0, 0.0))
    band_ref[...] = jnp.where((k < nz) & (n < nz), weight, 0.0).astype(jnp.bfloat16)

    pl.semaphore_wait(barrier, len(partners))

    sems = Sems(send_sem, recv_sem)
    sent = []
    size_p = 2 * n_rows // 3
    parts = []
    for turn in range(ROUNDS):
        root = coords(owner_ref[turn])
        parts.append(
            spread(
                orbital_ref.at[0], orbital_v, 0, size_p, psi[turn], land_p1[turn], land_p2[turn],
                held_p[turn], group_xy, group_z, root, sems, sent,
            )
        )
        parts.append(
            spread(
                orbital_ref.at[0], orbital_v, size_p, n_rows - size_p, psi[turn], land_q1[turn],
                land_q2[turn], held_q[turn], group_z, group_xy, root, sems, sent,
            )
        )

    def advance(turn):
        return [copy for part in parts[2 * turn : 2 * turn + 2] for copy in next(part, None) or ()]

    def swap_edges(ref, lead):
        every = (slice(None),) * lead
        first = ref.at[every + (pl.ds(PAD, HALO),)]
        last = ref.at[every + (pl.ds(PAD + nx - HALO, HALO),)]
        before = ref.at[every + (pl.ds(PAD - HALO, HALO),)]
        after = ref.at[every + (pl.ds(PAD + nx, HALO),)]
        copies = [
            remote(last, before, sems, cols, sec_right),
            remote(first, after, sems, cols, sec_left),
        ]
        for copy in copies:
            copy.start()
            sent.append(copy)
        return copies

    def turn_all(read, write):
        def one(y, carry):
            write(y, turned(read(y), nz))
            return carry

        lax.fori_loop(0, ny, one, 0, unroll=4)

    def put_d(y, value):
        d_t[y, PAD : PAD + nx, :] = 6.0 * (value - 1.0)

    sent += advance(0) + advance(1)
    loads[1].wait()
    turn_all(lambda y: potential_v[y], put_d)
    edges_in = swap_edges(d_t, 1)
    loads[2].wait()
    for column in range(2):
        def put_trial(y, value, column=column):
            trial_t[column, y, PAD : PAD + nx, :] = value

        turn_all(lambda y, column=column: trial_v[column, y], put_trial)
    edges_in += swap_edges(trial_t, 2)
    loads[0].wait()
    for turn in (0, 1, 0, 1):
        advance(turn)
    ahead = advance(0)
    for copy in edges_in:
        copy.wait_recv()
    for copy in ahead:
        copy.wait_send()
    sent += advance(1)

    def field_rows(turn, lo, hi):
        def one(block, carry):
            row = pl.multiple_of(block * 8, 8)
            for y in range(ny):
                value = psi_t[turn][y, pl.ds(row, 8), :]
                for column in range(2):
                    w[column, y, pl.ds(row, 8), :] = value * trial_t[column, y, pl.ds(row, 8), :]
            return carry

        lax.fori_loop(lo, hi, one, 0)

    def step_rows(src, dst, scale, sign, lo, hi):
        def one(block, carry):
            row = pl.multiple_of(8 * lo + block * BLOCK, 8)
            place = pl.ds(row, BLOCK)

            def store(c, y, v):
                base = scale * w[c, y, place, :]
                dst[c, y, place, :] = base + v if sign > 0 else base - v

            stencil(src, d_t, band_ref[...], (0, 1), ny, row, store)
            return carry

        lax.fori_loop(0, (hi - lo) * 8 // BLOCK, one, 0, unroll=2)

    def last_rows(turn, columns, lo, hi):
        def one(block, carry):
            row = pl.multiple_of(8 * lo + block * BLOCK, 8)
            place = pl.ds(pl.multiple_of(row - PAD, 8), BLOCK)

            def store(c, y, v):
                here = pl.ds(row, BLOCK)
                value = psi_t[turn][y, here, :] * (0.2 * w[c, y, here, :] + v * (1.0 / 864000.0))
                value = value[:, :nz]
                if turn > 0:
                    value = value + total[c, y, place, :]
                total[c, y, place, :] = value

            stencil(u2, d_t, band_ref[...], columns, ny, row, store)
            return carry

        lax.fori_loop(0, (hi - lo) * 8 // BLOCK, one, 0, unroll=2)

    a, b = PAD // 8, (PAD + nx) // 8

    def arrive(turn):
        def put_psi(y, value):
            psi_t[turn][y, PAD : PAD + nx, :] = value

        def get_psi(y):
            return psi[turn][pl.ds(pl.multiple_of(y * nz, 8), nz), :]

        advance(turn)
        turn_all(get_psi, put_psi)
        return swap_edges(psi_t[turn], 1)

    def first_two(turn, edges):
        field_rows(turn, a, b)
        step_rows(w, u1, 72.0, -1.0, a + 1, b - 1)
        for copy in edges:
            copy.wait_recv()
        field_rows(turn, a - 1, a)
        field_rows(turn, b, b + 1)
        step_rows(w, u1, 72.0, -1.0, a - 1, a + 1)
        step_rows(w, u1, 72.0, -1.0, b - 1, b + 1)
        step_rows(u1, u2, 3600.0, 1.0, a - 1, b + 1)

    first_two(0, arrive(0))
    edges = arrive(1)
    last_rows(0, (0, 1), a, b)
    first_two(1, edges)
    stores = []
    for part in range(PARTS):
        tall = nx // PARTS
        last_rows(1, (0, 1), a + part * tall // 8, a + (part + 1) * tall // 8)
        window = (slice(None), slice(None), pl.ds(part * tall, tall))
        store = pltpu.make_async_copy(total.at[window], out_ref.at[window], store_sem.at[part])
        store.start()
        stores.append(store)

    for copy in sent:
        copy.wait_send()
    for store in stores:
        store.wait()


def body(trial, orbitals, potential, owner):
    columns, ny, nz, nx = trial.shape
    n_rows = ny * nz
    tall = PAD + nx + PAD
    xy = X * H
    size_p, size_q = 2 * n_rows // 3, n_rows // 3
    any_spec = pl.BlockSpec(memory_space=pl.ANY)

    def each_round(*shape):
        return (pltpu.VMEM(shape, F32),) * ROUNDS

    n_sems = 4 * ROUNDS * (xy + Z - 2) + 2 * (2 + ROUNDS)
    out = pl.pallas_call(
        kernel,
        out_shape=jax.ShapeDtypeStruct((columns, ny, nx, nz), F32),
        in_specs=[pl.BlockSpec(memory_space=pltpu.SMEM), any_spec, any_spec, any_spec],
        out_specs=any_spec,
        scratch_shapes=[
            pltpu.VMEM(trial.shape, F32),
            pltpu.VMEM((n_rows, nx), F32),
            pltpu.VMEM((ny, nz, nx), F32),
            each_round(n_rows, nx),
            each_round(xy, size_p // xy, nx),
            each_round(Z, size_p // (xy * Z), nx),
            each_round(Z, size_q // Z, nx),
            each_round(xy, size_q // (xy * Z), nx),
            each_round(size_p // xy, nx),
            each_round(size_q // Z, nx),
            each_round(ny, tall, 128),
            pltpu.VMEM((columns, ny, tall, 128), F32),
            pltpu.VMEM((ny, tall, 128), F32),
            pltpu.VMEM((columns, ny, tall, 128), F32),
            pltpu.VMEM((columns, ny, tall, 128), F32),
            pltpu.VMEM((columns, ny, tall, 128), F32),
            pltpu.VMEM((columns, ny, nx, nz), F32),
            pltpu.VMEM((256, 128), jnp.bfloat16),
            pltpu.SemaphoreType.DMA((3,)),
            pltpu.SemaphoreType.DMA((PARTS,)),
            pltpu.SemaphoreType.DMA((n_sems,)),
            pltpu.SemaphoreType.DMA((n_sems,)),
        ],
        compiler_params=pltpu.CompilerParams(
            collective_id=0, has_side_effects=True, vmem_limit_bytes=60 * 1024 * 1024
        ),
    )(owner, trial, orbitals.reshape(orbitals.shape[0], n_rows, nx), potential)
    return out.transpose(0, 1, 3, 2)


def solution(mesh):
    placed = (P("cols", None, None, "sec"), P("cols", None, None, "sec"), P(None, None, "sec"), P())
    return jax.shard_map(
        body, mesh=mesh, in_specs=placed, out_specs=P("cols", None, None, "sec"), check_vma=False
    )
```

```python
import jax
import jax.numpy as jnp
from jax import lax
from jax.experimental import pallas as pl
from jax.experimental.pallas import tpu as pltpu
from jax.sharding import PartitionSpec as P

MESH = pl.DeviceIdType.MESH
F32 = jnp.float32

ROUNDS = 2
X, Z, H = 4, 8, 2
PAD = 16
PARTS = 4
BLOCK = 16
HALO = 8


def coords(index):
    return index // (Z * H), (index // H) % Z, index % H


def at(x, z, h):
    return (x * Z + z) * H + h


class Group:
    def __init__(self, name, me):
        self.name, self.me = name, me
        self.size = Z if name == "z" else X * H

    def shifted(self, offset):
        x, z, h = self.me
        if self.name == "z":
            return x, (z + offset) % Z, h
        return (x + offset // H) % X, z, (h + offset % H) % H

    def member(self, offset):
        return at(*self.shifted(offset))

    def place(self, offset=0):
        x, z, h = self.shifted(offset)
        return z if self.name == "z" else x * H + h

    def offset_of(self, root):
        x, z, h = self.me
        rx, rz, rh = root
        if self.name == "z":
            return (z - rz + Z) % Z
        return ((x - rx + X) % X) * H + (h - rh + H) % H


class Sems:
    def __init__(self, send, recv):
        self.send, self.recv, self.count = send, recv, 0

    def take(self):
        self.count += 1
        return self.send.at[self.count - 1], self.recv.at[self.count - 1]


def remote(src, dst, sems, cols, sec):
    send, recv = sems.take()
    return pltpu.make_async_remote_copy(
        src_ref=src, dst_ref=dst, send_sem=send, recv_sem=recv, device_id=(cols, sec), device_id_type=MESH
    )


def rows(ref, start, size):
    return ref.at[pl.ds(pl.multiple_of(start, 8), size), :]


def spread(first_copy, own, base, size, out, landed1, landed2, held, first, second, root, sems, sent):
    sec = lax.axis_index("sec")

    def go(src, dst, cols):
        copy = remote(src, dst, sems, cols, sec)
        copy.start()
        return copy

    def scatter(src, offset, piece, group, landed):
        return [
            go(rows(src, offset + group.place(k) * piece, piece), landed.at[k], group.member(k))
            for k in range(1, group.size)
        ]

    def taken(copies, src, offset, piece, group, landed):
        landed[0] = rows(src, offset + group.place() * piece, piece)[...]
        for copy in copies:
            copy.wait_recv()
        return landed[group.offset_of(root)]

    def gather(offset, piece, group):
        place = rows(out, offset + group.place() * piece, piece)
        return [go(place, place, group.member(k)) for k in range(1, group.size)]

    piece1 = size // first.size
    piece2 = piece1 // second.size
    inner = base + first.place() * piece1
    copies = scatter(first_copy, base, piece1, first, landed1)
    yield copies
    held[...] = taken(copies, own, base, piece1, first, landed1)
    copies = scatter(held, 0, piece2, second, landed2)
    sent += copies
    yield
    rows(out, inner + second.place() * piece2, piece2)[...] = taken(copies, held, 0, piece2, second, landed2)
    copies = gather(inner, piece2, second)
    sent += copies
    yield
    for copy in copies:
        copy.wait_recv()
    copies = gather(base, piece1, first)
    yield copies
    for copy in copies:
        copy.wait_recv()


def turned(plane, nz):
    return jnp.concatenate([plane, jnp.zeros((128 - nz, 128), F32)], axis=0).T


def along_lanes(fields, band):
    height = fields[0].shape[0]
    whole = jnp.concatenate(fields, axis=0)
    high = whole.astype(jnp.bfloat16)
    low = (whole - high.astype(F32)).astype(jnp.bfloat16)
    both = jnp.concatenate([high, low], axis=1)
    product = jnp.dot(both, band, preferred_element_type=F32)
    return [product[height * i : height * (i + 1), :] for i in range(len(fields))]


def stencil(src, d_ref, band, columns, ny, row, store):
    def read(column, plane, shift):
        return src[column, plane, pl.ds(row + shift, BLOCK), :]

    u = {(c, y): read(c, y, 0) for c in columns for y in range(ny)}
    lanes = dict(zip(u, along_lanes(list(u.values()), band)))
    for c, y in u:
        near = read(c, y, 1) + read(c, y, -1)
        far = read(c, y, 2) + read(c, y, -2)
        for shift in (-1, 1):
            if 0 <= y + shift < ny:
                near = near + u[c, y + shift]
        for shift in (-2, 2):
            if 0 <= y + shift < ny:
                far = far + u[c, y + shift]
        store(c, y, (far - 16.0 * near) + (lanes[c, y] + d_ref[y, pl.ds(row, BLOCK), :] * u[c, y]))


def kernel(
    owner_ref, trial_ref, orbital_ref, potential_ref, out_ref,
    trial_v, orbital_v, potential_v, psi, land_p1, land_p2, land_q1, land_q2, held_p, held_q,
    psi_t, trial_t, d_t, w, u1, u2, total, band_ref,
    load_sem, store_sem, send_sem, recv_sem,
):
    ny, nz, nx = potential_v.shape
    n_rows = ny * nz
    sec = lax.axis_index("sec")
    n_sec = lax.axis_size("sec")
    cols = lax.axis_index("cols")
    me = coords(cols)
    group_xy, group_z = Group("xy", me), Group("z", me)
    sec_right, sec_left = (sec + 1) % n_sec, (sec + n_sec - 1) % n_sec

    barrier = pltpu.get_barrier_semaphore()
    partners = [(g.member(k), sec) for g in (group_xy, group_z) for k in range(1, g.size)]
    partners += [(cols, sec_right), (cols, sec_left)]
    for partner in partners:
        pl.semaphore_signal(barrier, inc=1, device_id=partner, device_id_type=MESH)

    loads = [
        pltpu.make_async_copy(orbital_ref.at[0], orbital_v, load_sem.at[0]),
        pltpu.make_async_copy(potential_ref, potential_v, load_sem.at[1]),
        pltpu.make_async_copy(trial_ref, trial_v, load_sem.at[2]),
    ]
    for load in loads:
        load.start()

    k = lax.broadcasted_iota(jnp.int32, (256, 128), 0) % 128
    n = lax.broadcasted_iota(jnp.int32, (256, 128), 1)
    gap = jnp.abs(k - n)
    weight = jnp.where(gap == 1, -16.0, jnp.where(gap == 2, 1.0, 0.0))
    band_ref[...] = jnp.where((k < nz) & (n < nz), weight, 0.0).astype(jnp.bfloat16)

    pl.semaphore_wait(barrier, len(partners))

    sems = Sems(send_sem, recv_sem)
    sent = []
    size_p = 2 * n_rows // 3
    parts = []
    for turn in range(ROUNDS):
        root = coords(owner_ref[turn])
        parts.append(
            spread(
                orbital_ref.at[0], orbital_v, 0, size_p, psi[turn], land_p1[turn], land_p2[turn],
                held_p[turn], group_xy, group_z, root, sems, sent,
            )
        )
        parts.append(
            spread(
                orbital_ref.at[0], orbital_v, size_p, n_rows - size_p, psi[turn], land_q1[turn],
                land_q2[turn], held_q[turn], group_z, group_xy, root, sems, sent,
            )
        )

    def advance(turn):
        return [copy for part in parts[2 * turn : 2 * turn + 2] for copy in next(part, None) or ()]

    def swap_edges(ref, lead):
        every = (slice(None),) * lead
        first = ref.at[every + (pl.ds(PAD, HALO),)]
        last = ref.at[every + (pl.ds(PAD + nx - HALO, HALO),)]
        before = ref.at[every + (pl.ds(PAD - HALO, HALO),)]
        after = ref.at[every + (pl.ds(PAD + nx, HALO),)]
        copies = [
            remote(last, before, sems, cols, sec_right),
            remote(first, after, sems, cols, sec_left),
        ]
        for copy in copies:
            copy.start()
            sent.append(copy)
        return copies

    def turn_all(read, write):
        def one(y, carry):
            write(y, turned(read(y), nz))
            return carry

        lax.fori_loop(0, ny, one, 0, unroll=4)

    def put_d(y, value):
        d_t[y, PAD : PAD + nx, :] = 6.0 * (value - 1.0)

    sent += advance(0) + advance(1)
    loads[1].wait()
    turn_all(lambda y: potential_v[y], put_d)
    edges_in = swap_edges(d_t, 1)
    loads[2].wait()
    for column in range(2):
        def put_trial(y, value, column=column):
            trial_t[column, y, PAD : PAD + nx, :] = value

        turn_all(lambda y, column=column: trial_v[column, y], put_trial)
    edges_in += swap_edges(trial_t, 2)
    loads[0].wait()
    for turn in (0, 1, 0, 1):
        advance(turn)
    ahead = advance(0)
    for copy in edges_in:
        copy.wait_recv()
    for copy in ahead:
        copy.wait_send()
    sent += advance(1)

    def field_rows(turn, lo, hi):
        def one(block, carry):
            row = pl.multiple_of(8 * lo + block * 8, 8)
            for y in range(ny):
                value = psi_t[turn][y, pl.ds(row, 8), :]
                for column in range(2):
                    w[column, y, pl.ds(row, 8), :] = value * trial_t[column, y, pl.ds(row, 8), :]
            return carry

        lax.fori_loop(0, hi - lo, one, 0, unroll=2)

    def step_rows(src, dst, scale, sign, lo, hi):
        def one(block, carry):
            row = pl.multiple_of(8 * lo + block * BLOCK, 8)
            place = pl.ds(row, BLOCK)

            def store(c, y, v):
                base = scale * w[c, y, place, :]
                dst[c, y, place, :] = base + v if sign > 0 else base - v

            stencil(src, d_t, band_ref[...], (0, 1), ny, row, store)
            return carry

        lax.fori_loop(0, (hi - lo) * 8 // BLOCK, one, 0, unroll=3)

    def last_rows(turn, columns, lo, hi):
        def one(block, carry):
            row = pl.multiple_of(8 * lo + block * BLOCK, 8)
            place = pl.ds(pl.multiple_of(row - PAD, 8), BLOCK)

            def store(c, y, v):
                here = pl.ds(row, BLOCK)
                value = psi_t[turn][y, here, :] * (0.2 * w[c, y, here, :] + v * (1.0 / 864000.0))
                value = value[:, :nz]
                if turn > 0:
                    value = value + total[c, y, place, :]
                total[c, y, place, :] = value

            stencil(u2, d_t, band_ref[...], columns, ny, row, store)
            return carry

        lax.fori_loop(0, (hi - lo) * 8 // BLOCK, one, 0, unroll=2)

    a, b = PAD // 8, (PAD + nx) // 8

    def arrive(turn):
        def put_psi(y, value):
            psi_t[turn][y, PAD : PAD + nx, :] = value

        def get_psi(y):
            return psi[turn][pl.ds(pl.multiple_of(y * nz, 8), nz), :]

        advance(turn)
        turn_all(get_psi, put_psi)
        return swap_edges(psi_t[turn], 1)

    def first_two(turn, edges):
        field_rows(turn, a, b)
        step_rows(w, u1, 72.0, -1.0, a + 1, b - 1)
        for copy in edges:
            copy.wait_recv()
        field_rows(turn, a - 1, a)
        field_rows(turn, b, b + 1)
        step_rows(w, u1, 72.0, -1.0, a - 1, a + 1)
        step_rows(w, u1, 72.0, -1.0, b - 1, b + 1)
        step_rows(u1, u2, 3600.0, 1.0, a - 1, b + 1)

    first_two(0, arrive(0))
    edges = arrive(1)
    last_rows(0, (0, 1), a, b)
    first_two(1, edges)
    stores = []
    for part in range(PARTS):
        tall = nx // PARTS
        last_rows(1, (0, 1), a + part * tall // 8, a + (part + 1) * tall // 8)
        window = (slice(None), slice(None), pl.ds(part * tall, tall))
        store = pltpu.make_async_copy(total.at[window], out_ref.at[window], store_sem.at[part])
        store.start()
        stores.append(store)

    for copy in sent:
        copy.wait_send()
    for store in stores:
        store.wait()


def body(trial, orbitals, potential, owner):
    columns, ny, nz, nx = trial.shape
    n_rows = ny * nz
    tall = PAD + nx + PAD
    xy = X * H
    size_p, size_q = 2 * n_rows // 3, n_rows // 3
    any_spec = pl.BlockSpec(memory_space=pl.ANY)

    def each_round(*shape):
        return (pltpu.VMEM(shape, F32),) * ROUNDS

    n_sems = 4 * ROUNDS * (xy + Z - 2) + 2 * (2 + ROUNDS)
    out = pl.pallas_call(
        kernel,
        out_shape=jax.ShapeDtypeStruct((columns, ny, nx, nz), F32),
        in_specs=[pl.BlockSpec(memory_space=pltpu.SMEM), any_spec, any_spec, any_spec],
        out_specs=any_spec,
        scratch_shapes=[
            pltpu.VMEM(trial.shape, F32),
            pltpu.VMEM((n_rows, nx), F32),
            pltpu.VMEM((ny, nz, nx), F32),
            each_round(n_rows, nx),
            each_round(xy, size_p // xy, nx),
            each_round(Z, size_p // (xy * Z), nx),
            each_round(Z, size_q // Z, nx),
            each_round(xy, size_q // (xy * Z), nx),
            each_round(size_p // xy, nx),
            each_round(size_q // Z, nx),
            each_round(ny, tall, 128),
            pltpu.VMEM((columns, ny, tall, 128), F32),
            pltpu.VMEM((ny, tall, 128), F32),
            pltpu.VMEM((columns, ny, tall, 128), F32),
            pltpu.VMEM((columns, ny, tall, 128), F32),
            pltpu.VMEM((columns, ny, tall, 128), F32),
            pltpu.VMEM((columns, ny, nx, nz), F32),
            pltpu.VMEM((256, 128), jnp.bfloat16),
            pltpu.SemaphoreType.DMA((3,)),
            pltpu.SemaphoreType.DMA((PARTS,)),
            pltpu.SemaphoreType.DMA((n_sems,)),
            pltpu.SemaphoreType.DMA((n_sems,)),
        ],
        compiler_params=pltpu.CompilerParams(
            collective_id=0, has_side_effects=True, vmem_limit_bytes=60 * 1024 * 1024
        ),
    )(owner, trial, orbitals.reshape(orbitals.shape[0], n_rows, nx), potential)
    return out.transpose(0, 1, 3, 2)


def solution(mesh):
    placed = (P("cols", None, None, "sec"), P("cols", None, None, "sec"), P(None, None, "sec"), P())
    return jax.shard_map(
        body, mesh=mesh, in_specs=placed, out_specs=P("cols", None, None, "sec"), check_vma=False
    )
```
